32 devices in a mesh: rows: 8 (over y, x, core), chip: 4 (over z).
Axes of the slice: x: 2, y: 2, z: 4, core: 2. Of those that a mesh axis runs over, the one named last changes fastest.
Arguments:
- spectra: float32 [8192, 512], P(('rows', 'chip')), may hold values from -250 to 250
Outputs:
- whitened: float32 [8192, 512], P(('rows', 'chip'))
- triangle: float32 [512, 512], replicated
The draws below stay inside these ranges and needn't reach their ends.
All inputs are finite; a program needn't handle non-finite values.
Results may differ from the reference program's by a relative error of at most 0.000055.
Values sent between devices are 32-bit elements; how exact they have to be, the bound alone decides.
A program may use at most 64 MiB of HBM per device.

```python
import math
import jax
import jax.numpy as jnp
from jax import lax

N = 512
ROWS = 8192


def draw_spectra(key, part):
    keys = [jax.random.fold_in(key, 11 + number) for number in range(5)]
    column_scale = 0.5 * jnp.exp(jax.random.uniform(keys[1], (1, N), jnp.float32) * math.log(2.0))
    row_scale = 0.25 * jnp.exp(jax.random.uniform(keys[2], (ROWS, 1), jnp.float32) * math.log(10.0))
    trend = jnp.exp(jnp.arange(ROWS, dtype=jnp.float32)[:, None] * (math.log(3.0) / ROWS))
    common = jnp.clip(jax.random.normal(keys[3], (ROWS, 1), jnp.float32), -4.0, 4.0)
    base = jnp.clip(jax.random.normal(keys[0], (ROWS, N), jnp.float32), -6.0, 6.0)
    weights = jax.random.uniform(keys[4], (1, N), jnp.float32, 0.5, 1.5)
    mixed = 0.3 * common * weights + base
    return mixed * column_scale * row_scale * trend


def setup_inputs(seed: int = 0) -> dict:
    key_list = jax.random.split(jax.random.key(seed), 2)
    spectra = draw_spectra(jax.random.fold_in(key_list[1], 71), 0)
    return dict(spectra=spectra)


def reference(spectra):
    gram = lax.dot_general(spectra.astype(jnp.float32), spectra.astype(jnp.float32), (((0,), (0,)), ((), ())), precision=lax.Precision.HIGHEST, preferred_element_type=jnp.float32)
    lower = jnp.linalg.cholesky(gram)
    basis = lax.linalg.triangular_solve(lower, spectra, left_side=False, lower=True, transpose_a=True)
    factor_scale = math.sqrt(ROWS)
    return (basis * factor_scale, lower.T / factor_scale)
```

```python
import functools
import math

import jax
import jax.numpy as jnp
from jax import lax
from jax.experimental import pallas as pl
from jax.experimental.pallas import tpu as pltpu
from jax.sharding import PartitionSpec as P

WIDE = 128
SUB = 8
HIGHEST = lax.Precision.HIGHEST


def mm(a, b, dims):
    return lax.dot_general(
        a, b, (dims, ((), ())), precision=HIGHEST, preferred_element_type=jnp.float32
    )


def row_of(x, k):
    return jnp.broadcast_to(x[k : k + 1, :], (SUB, WIDE))


def lane_of(x, k):
    return jnp.broadcast_to(x[:, k : k + 1], (SUB, WIDE))


def factor_block(groups):
    count = len(groups)
    groups = list(groups)
    sub = lax.broadcasted_iota(jnp.int32, (SUB, WIDE), 0)
    lane = lax.broadcasted_iota(jnp.int32, (SUB, WIDE), 1)
    upper, inverse = [], []
    diag = [lane_of(groups[0], k) for k in range(SUB)]
    for g in range(count):
        p0 = g * SUB
        more = g + 1 < count
        own = (lane >= p0) & (lane < p0 + SUB)
        plain = groups[g]
        both = jnp.where(own, jnp.where(lane - p0 == sub, 1.0, 0.0), plain)
        full = both
        low = list(diag)
        jordan = list(diag)
        if more:
            after = [lane_of(groups[g + 1], p0 + k) for k in range(SUB)]
            ahead = [lane_of(groups[g + 1], p0 + SUB + k) for k in range(SUB)]
            after_low = list(after)
        for k in range(SUB):
            scale = lax.rsqrt(row_of(low[k], k))
            low_k = low[k] * scale
            times = [None] * SUB
            for j in range(k + 1, SUB):
                times[j] = row_of(low[j], k) * scale
            for j in range(k + 1, SUB):
                low[j] = low[j] - low_k * times[j]
            if more:
                after_k = after_low[k] * scale
                for j in range(k + 1, SUB):
                    after_low[j] = after_low[j] - after_k * times[j]
                for j in range(SUB):
                    ahead[j] = ahead[j] - after_k * row_of(after_k, j)
            below = jnp.where(sub > k, low_k, 0.0)
            at = sub == k
            plain_k = row_of(plain, k) * scale
            plain = jnp.where(at, plain_k, plain - below * plain_k)
            both_k = row_of(both, k) * scale
            both = jnp.where(at, both_k, both - below * both_k)
            if more:
                square = scale * scale
                full_k = row_of(full, k) * square
                full = jnp.where(at, full_k, full - jordan[k] * full_k)
                for j in range(k + 1, SUB):
                    t = row_of(jordan[j], k) * square
                    jordan[j] = jnp.where(at, t, jordan[j] - jordan[k] * t)
        upper.append(jnp.where(lane >= p0 + sub, jnp.where(own, plain, both), 0.0))
        inverse.append(jnp.where(lane <= p0 + sub, both, 0.0))
        if more:
            rows = [row_of(full, k) for k in range(SUB)]
            for q in range(g + 1, count):
                old = groups[q]
                new = jnp.where(own, 0.0, old)
                for k in range(SUB):
                    column = after[k] if q == g + 1 else lane_of(old, p0 + k)
                    new = new - column * rows[k]
                groups[q] = new
            diag = ahead
    return upper, inverse


def factor_kernel(row_scale, gram, spectra, whitened, triangle, work, held):
    n = gram.shape[0]
    blocks = n // WIDE
    groups = WIDE // SUB

    def at(i):
        return pl.ds(i * WIDE, WIDE)

    for p in range(blocks):
        source = gram if p == 0 else work
        rows = [
            source[p * WIDE + g * SUB : p * WIDE + (g + 1) * SUB, p * WIDE : (p + 1) * WIDE]
            for g in range(groups)
        ]
        upper, inverse = factor_block(rows)
        upper = jnp.concatenate(upper, axis=0)
        inverse = jnp.concatenate(inverse, axis=0)
        triangle[at(p), at(p)] = upper * (1.0 / row_scale)
        for q in range(p):
            triangle[at(p), at(q)] = jnp.zeros((WIDE, WIDE), jnp.float32)
        right = []
        for q in range(p + 1, blocks):
            block = mm(inverse, source[at(p), at(q)], ((1,), (0,)))
            right.append(block)
            triangle[at(p), at(q)] = block * (1.0 / row_scale)
            if q == p + 1:
                work[at(q), at(q)] = source[at(q), at(q)] - mm(block, block, ((0,), (0,)))
        for i, q in enumerate(range(p + 1, blocks)):
            for j, r in enumerate(range(p + 1, blocks)):
                if r < q or (q == p + 1 and r == q):
                    continue
                work[at(q), at(r)] = source[at(q), at(r)] - mm(right[i], right[j], ((0,), (0,)))
        slab = spectra if p == 0 else held
        basis = mm(slab[:, at(p)], inverse, ((1,), (1,)))
        whitened[:, at(p)] = basis * row_scale
        for i, q in enumerate(range(p + 1, blocks)):
            held[:, at(q)] = slab[:, at(q)] - mm(basis, right[i], ((1,), (0,)))


def factor(gram, spectra, total_rows):
    n = gram.shape[0]
    return pl.pallas_call(
        functools.partial(factor_kernel, math.sqrt(total_rows)),
        out_shape=(
            jax.ShapeDtypeStruct(spectra.shape, jnp.float32),
            jax.ShapeDtypeStruct((n, n), jnp.float32),
        ),
        in_specs=[pl.BlockSpec(memory_space=pltpu.VMEM)] * 2,
        out_specs=(pl.BlockSpec(memory_space=pltpu.VMEM),) * 2,
        scratch_shapes=[
            pltpu.VMEM((n, n), jnp.float32),
            pltpu.VMEM(spectra.shape, jnp.float32),
        ],
        compiler_params=pltpu.CompilerParams(vmem_limit_bytes=40 * 2**20),
    )(gram, spectra)


def summed_gram(block):
    gram = mm(block, block, ((0,), (0,)))
    band = lax.psum_scatter(gram, "rows", scatter_dimension=0, tiled=True)
    band = lax.psum(band, "chip")
    return lax.all_gather(band, "rows", axis=0, tiled=True)


def on_device(spectra):
    total_rows = lax.axis_size("rows") * lax.axis_size("chip") * spectra.shape[0]
    return factor(summed_gram(spectra), spectra, total_rows)


def solution(mesh):
    return jax.shard_map(
        on_device,
        mesh=mesh,
        in_specs=(P(("rows", "chip"), None),),
        out_specs=(P(("rows", "chip"), None), P()),
        check_vma=False,
    )
```

```python
import functools
import math

import jax
import jax.numpy as jnp
from jax import lax
from jax.experimental import pallas as pl
from jax.experimental.pallas import tpu as pltpu
from jax.sharding import PartitionSpec as P

WIDE = 128
SUB = 8
HIGHEST = lax.Precision.HIGHEST


def mm(a, b, dims):
    return lax.dot_general(
        a, b, (dims, ((), ())), precision=HIGHEST, preferred_element_type=jnp.float32
    )


def row_of(x, k):
    return jnp.broadcast_to(x[k : k + 1, :], (SUB, WIDE))


def lane_of(x, k):
    return jnp.broadcast_to(x[:, k : k + 1], (SUB, WIDE))


def factor_block(groups):
    count = len(groups)
    groups = list(groups)
    sub = lax.broadcasted_iota(jnp.int32, (SUB, WIDE), 0)
    lane = lax.broadcasted_iota(jnp.int32, (SUB, WIDE), 1)
    upper, inverse = [], []
    diag = [lane_of(groups[0], k) for k in range(SUB)]
    for g in range(count):
        p0 = g * SUB
        more = g + 1 < count
        own = (lane >= p0) & (lane < p0 + SUB)
        plain = groups[g]
        both = jnp.where(own, jnp.where(lane - p0 == sub, 1.0, 0.0), plain)
        full = both
        low = list(diag)
        jordan = list(diag)
        if more:
            after = [lane_of(groups[g + 1], p0 + k) for k in range(SUB)]
            ahead = [lane_of(groups[g + 1], p0 + SUB + k) for k in range(SUB)]
            after_low = list(after)
        for k in range(SUB):
            scale = lax.rsqrt(row_of(low[k], k))
            low_k = low[k] * scale
            times = [None] * SUB
            for j in range(k + 1, SUB):
                times[j] = row_of(low[j], k) * scale
            for j in range(k + 1, SUB):
                low[j] = low[j] - low_k * times[j]
            if more:
                after_k = after_low[k] * scale
                for j in range(k + 1, SUB):
                    after_low[j] = after_low[j] - after_k * times[j]
                for j in range(SUB):
                    ahead[j] = ahead[j] - after_k * row_of(after_k, j)
            below = jnp.where(sub > k, low_k, 0.0)
            at = sub == k
            plain_k = row_of(plain, k) * scale
            plain = jnp.where(at, plain_k, plain - below * plain_k)
            both_k = row_of(both, k) * scale
            both = jnp.where(at, both_k, both - below * both_k)
            if more:
                square = scale * scale
                full_k = row_of(full, k) * square
                full = jnp.where(at, full_k, full - jordan[k] * full_k)
                for j in range(k + 1, SUB):
                    t = row_of(jordan[j], k) * square
                    jordan[j] = jnp.where(at, t, jordan[j] - jordan[k] * t)
        upper.append(jnp.where(lane >= p0 + sub, jnp.where(own, plain, both), 0.0))
        inverse.append(jnp.where(lane <= p0 + sub, both, 0.0))
        if more:
            rows = [row_of(full, k) for k in range(SUB)]
            for q in range(g + 1, count):
                old = groups[q]
                new = jnp.where(own, 0.0, old)
                for k in range(SUB):
                    column = after[k] if q == g + 1 else lane_of(old, p0 + k)
                    new = new - column * rows[k]
                groups[q] = new
            diag = ahead
    return upper, inverse


def block_pairs(blocks):
    return [(i, j) for i in range(blocks) for j in range(i, blocks)]


def gram_kernel(sizes, spectra, out, packed, from_pair, halves, from_hi, sums, from_chip, *sems):
    pairs_n, chips, piece = sizes
    send_a, recv_a, send_b, recv_b, send_c, recv_c = sems[:6]
    send_gc, recv_gc, send_gb, recv_gb, send_ga, recv_ga, gathered = sems[6:]
    part = chips * piece
    half = pairs_n * part
    row, chip = lax.axis_index("rows"), lax.axis_index("chip")
    hi, lo = row // 2, row % 2
    other = (hi * 2 + 1 - lo, chip)

    def hi_at(d):
        return lax.rem(hi + d, pairs_n)

    def chip_at(d):
        return lax.rem(chip + d, chips)

    def hi_device(d):
        return (hi_at(d) * 2 + lo, chip)

    def chip_device(d):
        return (row, chip_at(d))

    def remote(src, dst, send, recv, device):
        return pltpu.make_async_remote_copy(
            src_ref=src, dst_ref=dst, send_sem=send, recv_sem=recv,
            device_id=device, device_id_type=pl.DeviceIdType.MESH,
        )

    barrier = pltpu.get_barrier_semaphore()
    partners = [other]
    partners += [hi_device(d) for d in range(1, pairs_n)]
    partners += [chip_device(d) for d in range(1, chips)]
    for device in partners:
        pl.semaphore_signal(barrier, inc=1, device_id=device, device_id_type=pl.DeviceIdType.MESH)

    n = spectra.shape[1]
    tiles = WIDE // SUB
    used = 0
    for i, j in block_pairs(n // WIDE):
        left = spectra[:, i * WIDE : (i + 1) * WIDE]
        right = spectra[:, j * WIDE : (j + 1) * WIDE]
        packed[used : used + tiles] = mm(left, right, ((0,), (0,))).reshape(tiles, SUB, WIDE)
        used += tiles
    if used < packed.shape[0]:
        packed[used:] = jnp.zeros((packed.shape[0] - used, SUB, WIDE), jnp.float32)
    pl.semaphore_wait(barrier, len(partners))

    started = []
    order = list(range(1, pairs_n)) + [0]
    pair_copies = {}
    for d in order:
        at = hi_at(d) * part
        copy = remote(
            packed.at[pl.ds((1 - lo) * half + at, part)], from_pair.at[d],
            send_a.at[d], recv_a.at[d], other,
        )
        copy.start()
        pair_copies[d] = copy
        started.append(copy)
    hi_copies = []
    for d in order:
        pair_copies[d].wait_recv()
        mine = packed[pl.ds(lo * half + hi_at(d) * part, part)] + from_pair[d]
        halves[d] = mine
        if d:
            copy = remote(halves.at[d], from_hi.at[d], send_b.at[d], recv_b.at[d], hi_device(d))
            copy.start()
            hi_copies.append(copy)
            started.append(copy)
    for copy in hi_copies:
        copy.wait_recv()
    chip_copies = []
    for d in list(range(1, chips)) + [0]:
        at = pl.ds(chip_at(d) * piece, piece)
        mine = halves[0, at]
        for e in range(1, pairs_n):
            mine = mine + from_hi[e, at]
        sums[d] = mine
        if d:
            copy = remote(sums.at[d], from_chip.at[d], send_c.at[d], recv_c.at[d], chip_device(d))
            copy.start()
            chip_copies.append(copy)
            started.append(copy)
    total = sums[0]
    for d, copy in enumerate(chip_copies, 1):
        copy.wait_recv()
        total = total + from_chip[d]

    own = (lo * pairs_n + hi) * part
    spot = gathered.at[pl.ds(own + chip * piece, piece)]
    gathered[pl.ds(own + chip * piece, piece)] = total
    gather_chip = []
    for d in range(1, chips):
        copy = remote(spot, spot, send_gc.at[d], recv_gc.at[d], chip_device(d))
        copy.start()
        gather_chip.append(copy)
    for copy in gather_chip:
        copy.wait_recv()
    started += gather_chip
    gather_hi = []
    spot = gathered.at[pl.ds(own, part)]
    for d in range(1, pairs_n):
        copy = remote(spot, spot, send_gb.at[d], recv_gb.at[d], hi_device(d))
        copy.start()
        gather_hi.append(copy)
    started += gather_hi
    gather_pair = []
    for d in range(pairs_n):
        source = lax.rem(hi + pairs_n - d, pairs_n)
        spot = gathered.at[pl.ds((lo * pairs_n + source) * part, part)]
        if d:
            gather_hi[d - 1].wait_recv()
        copy = remote(spot, spot, send_ga.at[d], recv_ga.at[d], other)
        copy.start()
        gather_pair.append(copy)
    for copy in gather_pair:
        copy.wait_recv()
    started += gather_pair
    out[...] = gathered[...]
    for copy in started:
        copy.wait_send()


def summed_gram(spectra):
    rows, chips = lax.axis_size("rows"), lax.axis_size("chip")
    pairs_n = rows // 2
    n = spectra.shape[1]
    used = len(block_pairs(n // WIDE)) * (WIDE // SUB)
    piece = -(-used // (rows * chips))
    part = piece * chips
    tiles = piece * rows * chips

    def tile_buffer(*lead):
        return pltpu.VMEM((*lead, SUB, WIDE), jnp.float32)

    sems = [
        pltpu.SemaphoreType.DMA((count,))
        for count in (pairs_n, pairs_n, chips, chips, pairs_n, pairs_n)
        for _ in range(2)
    ]
    return pl.pallas_call(
        functools.partial(gram_kernel, (pairs_n, chips, piece)),
        out_shape=jax.ShapeDtypeStruct((tiles, SUB, WIDE), jnp.float32),
        in_specs=[pl.BlockSpec(memory_space=pltpu.VMEM)],
        out_specs=pl.BlockSpec(memory_space=pltpu.VMEM),
        scratch_shapes=[
            tile_buffer(tiles),
            tile_buffer(pairs_n, part),
            tile_buffer(pairs_n, part),
            tile_buffer(pairs_n, part),
            tile_buffer(chips, piece),
            tile_buffer(chips, piece),
            *sems,
            tile_buffer(tiles),
        ],
        compiler_params=pltpu.CompilerParams(
            collective_id=0, has_side_effects=True, vmem_limit_bytes=40 * 2**20
        ),
    )(spectra)


def factor_kernel(row_scale, gram, spectra, whitened, triangle, work, held):
    n = spectra.shape[1]
    blocks = n // WIDE
    groups = WIDE // SUB

    def at(i):
        return pl.ds(i * WIDE, WIDE)

    place = {pair: k * groups for k, pair in enumerate(block_pairs(blocks))}

    def block_of(p, q, r):
        if p:
            return work[at(q), at(r)]
        first = place[q, r]
        return gram[first : first + groups].reshape(WIDE, WIDE)

    for p in range(blocks):
        diagonal = block_of(p, p, p)
        rows = [diagonal[g * SUB : (g + 1) * SUB] for g in range(groups)]
        upper, inverse = factor_block(rows)
        upper = jnp.concatenate(upper, axis=0)
        inverse = jnp.concatenate(inverse, axis=0)
        triangle[at(p), at(p)] = upper * (1.0 / row_scale)
        for q in range(p):
            triangle[at(p), at(q)] = jnp.zeros((WIDE, WIDE), jnp.float32)
        right = []
        for q in range(p + 1, blocks):
            block = mm(inverse, block_of(p, p, q), ((1,), (0,)))
            right.append(block)
            triangle[at(p), at(q)] = block * (1.0 / row_scale)
            if q == p + 1:
                work[at(q), at(q)] = block_of(p, q, q) - mm(block, block, ((0,), (0,)))
        for i, q in enumerate(range(p + 1, blocks)):
            for j, r in enumerate(range(p + 1, blocks)):
                if r < q or (q == p + 1 and r == q):
                    continue
                work[at(q), at(r)] = block_of(p, q, r) - mm(right[i], right[j], ((0,), (0,)))
        slab = spectra if p == 0 else held
        basis = mm(slab[:, at(p)], inverse, ((1,), (1,)))
        whitened[:, at(p)] = basis * row_scale
        for i, q in enumerate(range(p + 1, blocks)):
            held[:, at(q)] = slab[:, at(q)] - mm(basis, right[i], ((1,), (0,)))


def factor(gram, spectra, total_rows):
    n = spectra.shape[1]
    return pl.pallas_call(
        functools.partial(factor_kernel, math.sqrt(total_rows)),
        out_shape=(
            jax.ShapeDtypeStruct(spectra.shape, jnp.float32),
            jax.ShapeDtypeStruct((n, n), jnp.float32),
        ),
        in_specs=[pl.BlockSpec(memory_space=pltpu.VMEM)] * 2,
        out_specs=(pl.BlockSpec(memory_space=pltpu.VMEM),) * 2,
        scratch_shapes=[
            pltpu.VMEM((n, n), jnp.float32),
            pltpu.VMEM(spectra.shape, jnp.float32),
        ],
        compiler_params=pltpu.CompilerParams(vmem_limit_bytes=40 * 2**20),
    )(gram, spectra)


def on_device(spectra):
    total_rows = lax.axis_size("rows") * lax.axis_size("chip") * spectra.shape[0]
    return factor(summed_gram(spectra), spectra, total_rows)


def solution(mesh):
    return jax.shard_map(
        on_device,
        mesh=mesh,
        in_specs=(P(("rows", "chip"), None),),
        out_specs=(P(("rows", "chip"), None), P()),
        check_vma=False,
    )
```

```python
import functools
import math

import jax
import jax.numpy as jnp
from jax import lax
from jax.experimental import pallas as pl
from jax.experimental.pallas import tpu as pltpu
from jax.sharding import PartitionSpec as P

WIDE = 128
SUB = 8
HIGHEST = lax.Precision.HIGHEST


def mm(a, b, dims):
    return lax.dot_general(
        a, b, (dims, ((), ())), precision=HIGHEST, preferred_element_type=jnp.float32
    )


def row_of(x, k):
    return jnp.broadcast_to(x[k : k + 1, :], (SUB, WIDE))


def lane_of(x, k):
    return jnp.broadcast_to(x[:, k : k + 1], (SUB, WIDE))


def factor_block(groups, tick):
    count = len(groups)
    groups = list(groups)
    sub = lax.broadcasted_iota(jnp.int32, (SUB, WIDE), 0)
    lane = lax.broadcasted_iota(jnp.int32, (SUB, WIDE), 1)
    upper, inverse = [], []
    diag = [lane_of(groups[0], k) for k in range(SUB)]
    for g in range(count):
        tick()
        p0 = g * SUB
        more = g + 1 < count
        own = (lane >= p0) & (lane < p0 + SUB)
        plain = groups[g]
        both = jnp.where(own, jnp.where(lane - p0 == sub, 1.0, 0.0), plain)
        full = both
        low = list(diag)
        jordan = list(diag)
        if more:
            after = [lane_of(groups[g + 1], p0 + k) for k in range(SUB)]
            ahead = [lane_of(groups[g + 1], p0 + SUB + k) for k in range(SUB)]
            after_low = list(after)
        for k in range(SUB):
            scale = lax.rsqrt(row_of(low[k], k))
            low_k = low[k] * scale
            times = [None] * SUB
            for j in range(k + 1, SUB):
                times[j] = row_of(low[j], k) * scale
            for j in range(k + 1, SUB):
                low[j] = low[j] - low_k * times[j]
            if more:
                after_k = after_low[k] * scale
                for j in range(k + 1, SUB):
                    after_low[j] = after_low[j] - after_k * times[j]
                for j in range(SUB):
                    ahead[j] = ahead[j] - after_k * row_of(after_k, j)
            below = jnp.where(sub > k, low_k, 0.0)
            at = sub == k
            plain_k = row_of(plain, k) * scale
            plain = jnp.where(at, plain_k, plain - below * plain_k)
            both_k = row_of(both, k) * scale
            both = jnp.where(at, both_k, both - below * both_k)
            if more:
                square = scale * scale
                full_k = row_of(full, k) * square
                full = jnp.where(at, full_k, full - jordan[k] * full_k)
                for j in range(k + 1, SUB):
                    t = row_of(jordan[j], k) * square
                    jordan[j] = jnp.where(at, t, jordan[j] - jordan[k] * t)
        upper.append(jnp.where(lane >= p0 + sub, jnp.where(own, plain, both), 0.0))
        inverse.append(jnp.where(lane <= p0 + sub, both, 0.0))
        if more:
            rows = [row_of(full, k) for k in range(SUB)]
            for q in range(g + 1, count):
                old = groups[q]
                new = jnp.where(own, 0.0, old)
                for k in range(SUB):
                    column = after[k] if q == g + 1 else lane_of(old, p0 + k)
                    new = new - column * rows[k]
                groups[q] = new
            diag = ahead
    return upper, inverse


def chunk_blocks(blocks):
    rows = [[(i, j) for j in range(i, blocks)] for i in range(blocks)]
    chunks = [rows[0][:1], rows[0][1:], rows[1], sum(rows[2:], [])]
    return [chunk for chunk in chunks if chunk]


def chunk_sizes(n, row_count):
    tiles = WIDE // SUB
    return [-(-len(c) * tiles // row_count) for c in chunk_blocks(n // WIDE)]


def sum_chunk(pairs_n, chips, part, blocks, slab, bufs, sems, started):
    packed, from_pair, halves, from_hi, from_chip, gathered = bufs
    send, recv = sems
    half = pairs_n * part
    row, chip = lax.axis_index("rows"), lax.axis_index("chip")
    hi, lo = row // 2, row % 2
    other = (hi * 2 + 1 - lo, chip)
    tiles = WIDE // SUB
    order = list(range(1, pairs_n)) + [0]

    def hi_at(d):
        return lax.rem(hi + d, pairs_n)

    def remote(src, dst, slot, device):
        copy = pltpu.make_async_remote_copy(
            src_ref=src, dst_ref=dst, send_sem=send(slot), recv_sem=recv(slot),
            device_id=device, device_id_type=pl.DeviceIdType.MESH,
        )
        copy.start()
        started.append(copy)
        return copy

    slots = iter(range(4 * pairs_n + chips))
    used = 0
    for i, j in blocks:
        left = slab[:, i * WIDE : (i + 1) * WIDE]
        right = slab[:, j * WIDE : (j + 1) * WIDE]
        packed[used : used + tiles] = mm(left, right, ((0,), (0,))).reshape(tiles, SUB, WIDE)
        used += tiles
    if used < 2 * half:
        packed[used:] = jnp.zeros((2 * half - used, SUB, WIDE), jnp.float32)
    yield
    pair_copies = {}
    for d in order:
        source = packed.at[pl.ds((1 - lo) * half + hi_at(d) * part, part)]
        pair_copies[d] = remote(source, from_pair.at[d], next(slots), other)
    yield
    copies = []
    for d in order:
        pair_copies[d].wait_recv()
        mine = packed[pl.ds(lo * half + hi_at(d) * part, part)] + from_pair[d]
        halves[d] = mine
        if d:
            device = (hi_at(d) * 2 + lo, chip)
            copies.append(remote(halves.at[d], from_hi.at[d], next(slots), device))
    yield
    for copy in copies:
        copy.wait_recv()
    mine = halves[0]
    for d in range(1, pairs_n):
        mine = mine + from_hi[d]
    from_chip[chip] = mine
    spot = from_chip.at[chip]
    copies = [
        remote(spot, spot, next(slots), (row, lax.rem(chip + d, chips)))
        for d in range(1, chips)
    ]
    yield
    for copy in copies:
        copy.wait_recv()
    total = from_chip[0]
    for c in range(1, chips):
        total = total + from_chip[c]
    own = pl.ds((lo * pairs_n + hi) * part, part)
    gathered[own] = total
    spot = gathered.at[own]
    hi_copies = [
        remote(spot, spot, next(slots), (hi_at(d) * 2 + lo, chip))
        for d in range(1, pairs_n)
    ]
    copies = [remote(spot, spot, next(slots), other)]
    yield
    for d in range(1, pairs_n):
        source = lax.rem(hi + pairs_n - d, pairs_n)
        spot = gathered.at[pl.ds((lo * pairs_n + source) * part, part)]
        hi_copies[d - 1].wait_recv()
        copies.append(remote(spot, spot, next(slots), other))
    yield
    for copy in copies:
        copy.wait_recv()


BEFORE = (0, 1, 0, 2, 1, 0, 3, 2, 0, 1, 3, 0, 2, 0)
DURING = (1, 3, 2, 1, 3, 1, 2, 2, 3, 3)


def kernel(sizes, spectra, whitened, triangle, upper, held, send, recv, *bufs):
    row_scale, pairs_n, chips, parts = sizes
    n = spectra.shape[1]
    blocks = n // WIDE
    groups = WIDE // SUB
    row, chip = lax.axis_index("rows"), lax.axis_index("chip")
    hi, lo = row // 2, row % 2

    def at(i):
        return pl.ds(i * WIDE, WIDE)

    barrier = pltpu.get_barrier_semaphore()
    partners = [(hi * 2 + 1 - lo, chip)]
    partners += [(lax.rem(hi + d, pairs_n) * 2 + lo, chip) for d in range(1, pairs_n)]
    partners += [(row, lax.rem(chip + d, chips)) for d in range(1, chips)]
    for device in partners:
        pl.semaphore_signal(barrier, inc=1, device_id=device, device_id_type=pl.DeviceIdType.MESH)

    started = []
    chunks = chunk_blocks(blocks)
    sums, place = [], {}
    for c, (pairs, part) in enumerate(zip(chunks, parts)):
        mine = bufs[6 * c : 6 * c + 6]
        sems = (lambda s, c=c: send.at[c, s], lambda s, c=c: recv.at[c, s])
        sums.append(sum_chunk(pairs_n, chips, part, pairs, spectra, mine, sems, started))
        for k, pair in enumerate(pairs):
            place[pair] = (mine[5], k * groups)
    next(sums[0])
    pl.semaphore_wait(barrier, len(partners))
    next(sums[0])

    def advance(c):
        next(sums[c], None)

    entered = {0}
    for c in BEFORE[1:]:
        if c not in entered:
            entered.add(c)
            advance(c)
        advance(c)
    todo = list(DURING)

    def tick():
        if todo:
            advance(todo.pop(0))

    def gram(q, r):
        buf, first = place[q, r]
        return buf[first : first + groups].reshape(WIDE, WIDE)

    def less_above(p, q, r):
        block = gram(q, r)
        if p:
            above = pl.ds(0, p * WIDE)
            block = block - mm(upper[above, at(q)], upper[above, at(r)], ((0,), (0,)))
        return block

    diagonal = gram(0, 0)
    slab = spectra[:, at(0)]
    for p in range(blocks):
        rest = range(p + 1, blocks)
        ahead = {q: less_above(p, p, q) for q in rest} if p else {}
        corner = less_above(p, p + 1, p + 1) if p and rest else None
        if p:
            above = pl.ds(0, p * WIDE)
            slab = spectra[:, at(p)] - mm(held[:, above], upper[above, at(p)], ((1,), (0,)))
        rows = [diagonal[g * SUB : (g + 1) * SUB] for g in range(groups)]
        own, inverse = factor_block(rows, tick)
        while todo:
            tick()
        if p == 0:
            ahead = {q: gram(0, q) for q in rest}
            corner = gram(1, 1) if rest else None
        inverse = jnp.concatenate(inverse, axis=0)
        for q in rest:
            block = mm(inverse, ahead[q], ((1,), (0,)))
            upper[at(p), at(q)] = block
            triangle[at(p), at(q)] = block * (1.0 / row_scale)
            if q == p + 1:
                diagonal = corner - mm(block, block, ((0,), (0,)))
        triangle[at(p), at(p)] = jnp.concatenate(own, axis=0) * (1.0 / row_scale)
        for q in range(p):
            triangle[at(p), at(q)] = jnp.zeros((WIDE, WIDE), jnp.float32)
        basis = mm(slab, inverse, ((1,), (1,)))
        held[:, at(p)] = basis
        whitened[:, at(p)] = basis * row_scale
    for copy in started:
        copy.wait_send()


def on_device(spectra):
    rows, chips = lax.axis_size("rows"), lax.axis_size("chip")
    pairs_n = rows // 2
    n = spectra.shape[1]
    parts = chunk_sizes(n, rows)
    row_scale = math.sqrt(rows * chips * spectra.shape[0])

    def tiles(*lead):
        return pltpu.VMEM((*lead, SUB, WIDE), jnp.float32)

    bufs = []
    for part in parts:
        bufs += [
            tiles(rows * part),
            tiles(pairs_n, part),
            tiles(pairs_n, part),
            tiles(pairs_n, part),
            tiles(chips, part),
            tiles(rows * part),
        ]
    sems = pltpu.SemaphoreType.DMA((len(parts), 4 * pairs_n + chips))
    return pl.pallas_call(
        functools.partial(kernel, (row_scale, pairs_n, chips, parts)),
        out_shape=(
            jax.ShapeDtypeStruct(spectra.shape, jnp.float32),
            jax.ShapeDtypeStruct((n, n), jnp.float32),
        ),
        in_specs=[pl.BlockSpec(memory_space=pltpu.VMEM)],
        out_specs=(pl.BlockSpec(memory_space=pltpu.VMEM),) * 2,
        scratch_shapes=[
            pltpu.VMEM((n, n), jnp.float32),
            pltpu.VMEM(spectra.shape, jnp.float32),
            sems,
            sems,
            *bufs,
        ],
        compiler_params=pltpu.CompilerParams(
            collective_id=0, has_side_effects=True, vmem_limit_bytes=40 * 2**20
        ),
    )(spectra)


def solution(mesh):
    return jax.shard_map(
        on_device,
        mesh=mesh,
        in_specs=(P(("rows", "chip"), None),),
        out_specs=(P(("rows", "chip"), None), P()),
        check_vma=False,
    )
```
